32 devices in a mesh: groups: 2 (over x), ctx: 16 (over z, y, core).
Axes of the slice: x: 2, y: 2, z: 4, core: 2. Of those that a mesh axis runs over, the one named last changes fastest.
Arguments:
- tokens: bfloat16 [16384, 2048], P(('groups', 'ctx')), parts along dimension 0, may hold values from -14 to 14, as said below
- projected: bfloat16 [16384, 6144], P(('groups', 'ctx')), parts along dimension 0, may hold values from -6 to 6
- short_filter: float32 [3, 6144], replicated, may hold values from -3 to 3
- long_filter: bfloat16 [128, 128], replicated, may hold values from -0.5 to 0.5
- conv_bias: float32 [2048], replicated, may hold values from 0.5 to 1.5
- out_weight: bfloat16 [2048, 2048], P(None, 'ctx'), may hold values from -0.125 to 0.125
Outputs:
- result: bfloat16 [16384, 2048], P(('groups', 'ctx')), parts along dimension 0
The draws below stay inside these ranges and needn't reach their ends.
There are 2 independent parts, one for each index of `groups`. The reference program is written for one: setup_inputs(seed, part) draws one part's arguments, and reference() takes and returns one part's arrays. A program takes and returns all parts, laid end to end along the dimension named above; an argument that names none is the same for every part. Nothing has to cross between parts.
Inputs may be any that keep to these rules, and one draw needn't show every extreme that they name: `tokens`: activations of the residual stream.
All inputs are finite; a program needn't handle non-finite values.
Results may differ from the reference program's by a relative error of at most 0.012.
Values may be sent and summed in bfloat16 or wider, within the bound.
A program may use at most 128 MiB of HBM per device.

```python
import jax
import jax.numpy as jnp
from jax import lax

D = 2048
CH = 2048
GROUP = 16
GROUPS = 128
SHORT = 3
KLEN = 128
LENGTH = 8192


def draw_tokens(key, part):
    base = jnp.clip(jax.random.normal(jax.random.fold_in(key, 3), (LENGTH, D), jnp.float32), -6.0, 6.0)
    return base.astype(jnp.bfloat16)


def steps_of(rng, extent, shards, least, high):
    def one(dim, blocks):
        steps = jax.random.uniform(jax.random.fold_in(jax.random.fold_in(rng, 6), dim), (blocks,), jnp.float32, least / len(shards), high / len(shards))
        return jnp.repeat(jnp.exp(steps), extent[dim] // blocks).reshape((-1,) + (1,) * (len(extent) - dim - 1))

    gain = one(*shards[0])
    for cut in shards[1:]:
        gain = gain * one(*cut)
    return gain


def bell_draw(own_key, extent, spread, most, pieces=(), held_as=jnp.bfloat16):
    entries = spread * jax.random.normal(own_key, extent, jnp.float32)
    if pieces:
        entries = entries * steps_of(own_key, extent, pieces, -0.22, 0.18)
    return jnp.clip(entries, -most, most).astype(held_as)


def setup_inputs(seed: int = 0, part: int = 0) -> dict:
    splits = jax.random.split(jax.random.key(seed), 7)
    part_keys = jax.random.split(jax.random.fold_in(splits[6], part), 7)
    return {
        "tokens": draw_tokens(jax.random.fold_in(jax.random.fold_in(splits[6], part), 71), part),
        "projected": bell_draw(part_keys[1], (LENGTH, 3 * CH), 1.0, 6.0, ((0, 16),)),
        "short_filter": bell_draw(splits[2], (SHORT, 3 * CH), 0.6, 3.0, (), jnp.float32),
        "long_filter": bell_draw(splits[3], (GROUPS, KLEN), KLEN ** -0.5, 0.5),
        "conv_bias": jnp.clip(jax.random.uniform(splits[4], (CH,), jnp.float32, 0.5, 1.5), 0.5, 1.5),
        "out_weight": bell_draw(splits[5], (CH, D), CH ** -0.5, 0.125, ((1, 16),)),
    }


def reference(tokens, projected, short_filter, long_filter, conv_bias, out_weight):
    padded = jnp.concatenate([jnp.zeros((2, 3 * CH), jnp.bfloat16), projected], axis=0).astype(jnp.float32)
    mixed = short_filter[0] * padded[2:] + short_filter[1] * padded[1:-1] + short_filter[2] * padded[:-2]
    gate_rows = mixed[:, :CH]
    carried = (mixed[:, CH:2 * CH] * mixed[:, 2 * CH:]).astype(jnp.bfloat16)
    carried_pad = jnp.concatenate([jnp.zeros((KLEN - 1, CH), jnp.bfloat16), carried], axis=0)
    channel_taps = jnp.repeat(long_filter.astype(jnp.float32), GROUP, axis=0)

    def add_tap(step, total):
        offset = (KLEN - 1 - step).astype(jnp.int32)
        window = lax.dynamic_slice_in_dim(carried_pad, offset, LENGTH, 0).astype(jnp.float32)
        tap = lax.dynamic_index_in_dim(channel_taps, step.astype(jnp.int32), 1, keepdims=False)
        return total + window * tap[None, :]

    conv = lax.fori_loop(0, KLEN, add_tap, jnp.zeros((LENGTH, CH), jnp.float32))
    gated = (gate_rows * (conv + conv_bias * carried.astype(jnp.float32))).astype(jnp.bfloat16)
    branch = jnp.dot(gated, out_weight, preferred_element_type=jnp.float32)
    return (tokens.astype(jnp.float32) + branch).astype(jnp.bfloat16)
```

```python
import functools

import jax
import jax.numpy as jnp
from jax import lax
from jax.experimental import pallas as pl
from jax.experimental.pallas import tpu as pltpu
from jax.sharding import PartitionSpec as P

F32 = jnp.float32
BF16 = jnp.bfloat16
MESH = pl.DeviceIdType.MESH
LANES = 128
CHUNK = 256
EDGE = 16
SIDE = 608


def layer_kernel(
    tok, proj, sf, lf, cb, w, out,
    pv, xv, xr, tv, hr, wv, gv, tk, ob,
    ring_s, ring_r, x_s, x_r, sib_s, sib_r, halo_s, halo_r, loc, out_s,
):
    rows, channels = tok.shape[0], w.shape[0]
    taps = lf.shape[1]
    chunks = channels // CHUNK
    middle = channels - 2 * SIDE
    shard = w.shape[1]

    grp = lax.axis_index("groups")
    me = lax.axis_index("ctx")
    devices = lax.axis_size("ctx")
    core = me % 2
    chip = me // 2
    ring = devices // 2
    depth = ring // 2
    cz, cy = chip // 2, chip % 2
    pos = cz * (1 - cy) + (ring - 1 - cz) * cy

    def chip_at(position):
        q = (position + ring) % ring
        qy = q // depth
        qz = q * (1 - qy) + (ring - 1 - q) * qy
        return qz * 2 + qy

    def device_at(position):
        return chip_at(position) * 2 + core

    right = (grp, device_at(pos + 1))
    left = (grp, device_at(pos - 1))
    across = (1 - grp, me)
    sibling = (grp, me + 1 - 2 * core)
    following = (grp, (me + 1) % devices)
    previous = (grp, (me + devices - 1) % devices)
    has_next = me < devices - 1
    has_prev = me > 0

    tail = taps + EDGE
    head = rows - tail
    load_tail = pltpu.make_async_copy(proj.at[pl.ds(head, tail)], pv.at[pl.ds(EDGE + head, tail)], loc.at[0])
    load_head = pltpu.make_async_copy(proj.at[pl.ds(0, head)], pv.at[pl.ds(EDGE, head)], loc.at[1])
    load_tok = pltpu.make_async_copy(tok, tk, loc.at[2])
    load_w = pltpu.make_async_copy(w, wv.at[me], loc.at[3])
    load_tail.start()
    load_head.start()
    load_w.start()
    load_tok.start()

    barrier = pltpu.get_barrier_semaphore()
    for other in (left, right, across, sibling, following, previous):
        pl.semaphore_signal(barrier, inc=1, device_id=other, device_id_type=MESH)
    pl.semaphore_wait(barrier, 6)

    def remote(src, dst, ssem, rsem, dev):
        return pltpu.make_async_remote_copy(
            src_ref=src, dst_ref=dst, send_sem=ssem, recv_sem=rsem, device_id=dev, device_id_type=MESH
        )

    def span(step, d, piece):
        size = middle if piece == 1 else SIDE
        if piece == 0:
            start = grp * (SIDE + middle)
        elif piece == 1:
            start = SIDE
        else:
            start = (1 - grp) * (SIDE + middle)
        if step == depth:
            size = size // 2
            start = start + d * size
        return pl.ds(pl.multiple_of(start, EDGE), size)

    def owner(step, d):
        return device_at(pos - step) if d == 0 else device_at(pos + step)

    def ring_copy(step, d, piece):
        own = owner(step - 1, d)
        sp = span(step, d, piece)
        i = (step - 1) * 4 + d * 2 + piece
        src = w.at[sp] if step == 1 else wv.at[own, sp]
        return remote(src, wv.at[own, sp], ring_s.at[i], ring_r.at[i], right if d == 0 else left)

    def across_copy(step, d, piece=0):
        own = owner(step, d)
        sp = span(step, d, piece)
        i = (step - 1) * 2 + d
        return remote(wv.at[own, sp], wv.at[own, sp], x_s.at[i], x_r.at[i], across)

    def sibling_copy(step, d, piece):
        own = owner(step, d)
        sp = span(step, d, piece)
        i = (step - 1) * 6 + d * 3 + piece
        return remote(wv.at[own, sp], wv.at[own, sp], sib_s.at[i], sib_r.at[i], sibling)

    own_sib = remote(w, wv.at[me], sib_s.at[depth * 6], sib_r.at[depth * 6], sibling)
    edge_copy = remote(
        proj.at[pl.ds(rows - EDGE, EDGE)], pv.at[pl.ds(0, EDGE)], halo_s.at[0], halo_r.at[0], following
    )
    halo_copy = remote(
        xv.at[pl.ds(rows, taps)], xv.at[pl.ds(0, taps)], halo_s.at[1], halo_r.at[1], following
    )

    def ring_arrival(step, d, piece):
        own = owner(step, d)
        sp = span(step, d, piece)
        i = (step - 1) * 4 + d * 2 + piece
        remote(wv.at[own, sp], wv.at[own, sp], ring_s.at[i], ring_r.at[i], right).wait_recv()
        if step < depth:
            ring_copy(step + 1, d, piece).start()
        if piece == 0:
            across_copy(step, d).start()
        sibling_copy(step, d, piece).start()

    def across_arrival(step, d):
        across_copy(step, d, 2).wait_recv()
        sibling_copy(step, d, 2).start()

    @pl.when(has_next)
    def _():
        edge_copy.start()

    for piece in (0, 1):
        for d in (0, 1):
            ring_copy(1, d, piece).start()
    own_sib.start()

    def ring_both(step, piece):
        ring_arrival(step, 0, piece)
        ring_arrival(step, 1, piece)

    def across_both(step):
        across_arrival(step, 0)
        across_arrival(step, 1)

    def at(index, k, *events):
        @pl.when(k == index)
        def _():
            for fn, *args in events:
                fn(*args)

    def mix(r0, count, c0, width):
        cols = pl.ds(pl.multiple_of(c0, LANES), width)
        x = pv[pl.ds(pl.multiple_of(r0, EDGE), count + EDGE), cols].astype(F32)
        total = sf[0:1, cols] * x[EDGE:]
        total = total + sf[1:2, cols] * x[EDGE - 1 : -1]
        return total + sf[2:3, cols] * x[EDGE - 2 : -2]

    strip = 64

    def carry_strip(r0, c0):
        prod = mix(r0, strip, channels + c0, LANES) * mix(r0, strip, 2 * channels + c0, LANES)
        at_rows = pl.ds(pl.multiple_of(taps + r0, EDGE), strip)
        cols = pl.ds(pl.multiple_of(c0, LANES), LANES)
        xv[at_rows, cols] = prod.astype(BF16)
        xr[at_rows, cols] = pltpu.roll(prod, LANES // 2, 1).astype(BF16)

    load_tail.wait()
    tiles = channels // LANES

    @pl.loop(0, tiles)
    def _(t):
        for r in range(rows - taps, rows, strip):
            carry_strip(r, t * LANES)

    @pl.when(has_next)
    def _():
        halo_copy.start()

    jj = lax.broadcasted_iota(jnp.int32, (taps, 2 * taps), 0)
    ss = lax.broadcasted_iota(jnp.int32, (taps, 2 * taps), 1)
    flip = jnp.where(ss == taps - jj, 1.0, 0.0).astype(BF16)
    hr[...] = jnp.dot(lf[...], flip, preferred_element_type=F32)

    @pl.when(me == 0)
    def _():
        pv[0:EDGE, :] = jnp.zeros((EDGE, pv.shape[1]), BF16)
        xv[0:taps, :] = jnp.zeros((taps, channels), BF16)

    @pl.when(has_prev)
    def _():
        edge_copy.wait_recv()

    load_head.wait()

    def build_taps(g):
        row = jnp.broadcast_to(hr[pl.ds(g, 1), :], (taps, 2 * taps))
        mat = pltpu.roll(row, 0, 1, stride=1, stride_axis=0)
        tv[pl.ds(pl.multiple_of(g * taps, taps), taps), :] = mat.astype(BF16)

    per_tile = lf.shape[0] // tiles

    @pl.loop(0, tiles)
    def _(t):
        for r in range(0, rows - taps, strip):
            carry_strip(r, t * LANES)

        @pl.loop(0, per_tile)
        def _(i):
            build_taps(t * per_tile + i)

        at(7, t, (ring_both, 1, 0))
        at(13, t, (ring_both, 1, 1))

    @pl.when(has_prev)
    def _():
        halo_copy.wait_recv()

    half = LANES // 2
    quarter = per_tile // 2
    gw = half // quarter
    pairs = rows // (2 * taps)
    low = lax.broadcasted_iota(jnp.int32, (1, LANES), 1) < half

    def conv_tile(t):
        c0 = t * LANES
        cols = pl.ds(pl.multiple_of(c0, LANES), LANES)
        lows, highs = [], []
        for j in range(pairs):
            a = xv[pl.ds(j * 2 * taps, 2 * taps), cols]
            b = xr[pl.ds(j * 2 * taps + taps, 2 * taps), cols]
            lows.append(jnp.where(low, a, b))
            highs.append(jnp.where(low, b, a))
        parts = []
        lane = lax.broadcasted_iota(jnp.int32, (1, pairs * LANES), 1)
        which = (lane % half) // gw
        for side, blocks in enumerate((lows, highs)):
            rhs = jnp.concatenate(blocks, axis=1)
            first = (t * per_tile + side * quarter) * taps
            res = jnp.dot(
                tv[pl.ds(pl.multiple_of(first, taps), quarter * taps), :], rhs, preferred_element_type=F32
            )
            total = res[0:taps]
            for i in range(1, quarter):
                total = jnp.where(which == i, res[i * taps : (i + 1) * taps], total)
            parts.append(total)
        for j in range(pairs):
            z1 = parts[0][:, j * LANES : (j + 1) * LANES]
            z2 = parts[1][:, j * LANES : (j + 1) * LANES]
            even = jnp.where(low, z1, z2)
            odd = pltpu.roll(jnp.where(low, z2, z1), half, 1)
            for b, conv in ((2 * j, even), (2 * j + 1, odd)):
                r0 = b * taps
                carried = xv[pl.ds(taps + r0, taps), cols].astype(F32)
                gate = mix(r0, taps, c0, LANES)
                gv[pl.ds(r0, taps), cols] = (gate * (conv + cb[0:1, cols] * carried)).astype(BF16)

    @pl.loop(0, tiles)
    def _(t):
        conv_tile(t)
        at(1, t, (across_both, 1))
        at(4, t, (ring_both, 2, 0))
        at(8, t, (ring_both, 2, 1))
        at(11, t, (across_both, 2))
        at(14, t, (ring_both, 3, 0))

    load_tok.wait()
    load_w.wait()

    def sibling_wait(step, d):
        for piece in range(3):
            sibling_copy(step, d, piece).wait_recv()

    blocks = ring
    width = 2 * shard

    def out_copy(idx):
        sign = 1 - 2 * (idx % 2)
        c = chip_at(pos + ((idx + 1) // 2) * sign)
        cols = pl.ds(pl.multiple_of(c * width, width), width)
        return pltpu.make_async_copy(ob.at[:, cols], out.at[:, cols], out_s.at[idx])

    @pl.loop(0, blocks)
    def _(idx):
        at(0, idx, (own_sib.wait_recv,))
        at(1, idx, (sibling_wait, 1, 0))
        at(2, idx, (sibling_wait, 1, 1), (ring_both, 3, 1))
        at(3, idx, (sibling_wait, 2, 0))
        at(4, idx, (sibling_wait, 2, 1), (across_both, 3), (ring_both, 4, 0), (ring_both, 4, 1))
        at(5, idx, (sibling_wait, 3, 0))
        at(6, idx, (sibling_wait, 3, 1), (across_both, 4))
        at(7, idx, (sibling_wait, depth, 0), (sibling_wait, depth, 1))
        sign = 1 - 2 * (idx % 2)
        c = chip_at(pos + ((idx + 1) // 2) * sign)
        cols = pl.ds(pl.multiple_of(c * width, width), width)

        rhs = jnp.concatenate([wv[2 * c], wv[2 * c + 1]], axis=1)
        branch = jnp.dot(gv[...], rhs, preferred_element_type=F32)
        ob[:, cols] = (tk[:, cols].astype(F32) + branch).astype(BF16)
        out_copy(idx).start()

    for step in range(1, depth + 1):
        for d in (0, 1):
            ring_copy(step, d, 0).wait_send()
            ring_copy(step, d, 1).wait_send()
            across_copy(step, d).wait_send()
            for piece in range(3):
                sibling_copy(step, d, piece).wait_send()
    own_sib.wait_send()

    @pl.when(has_next)
    def _():
        edge_copy.wait_send()
        halo_copy.wait_send()

    for idx in range(blocks):
        out_copy(idx).wait()


def on_device(tokens, projected, short_filter, long_filter, conv_bias, out_weight):
    rows, channels = tokens.shape[0], out_weight.shape[0]
    taps = long_filter.shape[1]
    devices = lax.axis_size("ctx")
    chips = devices // 2
    depth = chips // 2
    anyspace = pl.BlockSpec(memory_space=pl.ANY)
    vmem = pl.BlockSpec(memory_space=pltpu.VMEM)
    dma = pltpu.SemaphoreType.DMA
    return pl.pallas_call(
        layer_kernel,
        out_shape=jax.ShapeDtypeStruct(tokens.shape, BF16),
        in_specs=[anyspace, anyspace, vmem, vmem, vmem, anyspace],
        out_specs=anyspace,
        scratch_shapes=[
            pltpu.VMEM((rows + EDGE, projected.shape[1]), BF16),
            pltpu.VMEM((rows + taps, channels), BF16),
            pltpu.VMEM((rows + taps, channels), BF16),
            pltpu.VMEM((long_filter.shape[0] * taps, 2 * taps), BF16),
            pltpu.VMEM((long_filter.shape[0], 2 * taps), F32),
            pltpu.VMEM((devices, channels, out_weight.shape[1]), BF16),
            pltpu.VMEM((rows, channels), BF16),
            pltpu.VMEM(tokens.shape, BF16),
            pltpu.VMEM(tokens.shape, BF16),
            dma((depth * 4,)),
            dma((depth * 4,)),
            dma((depth * 2,)),
            dma((depth * 2,)),
            dma((depth * 6 + 1,)),
            dma((depth * 6 + 1,)),
            dma((2,)),
            dma((2,)),
            dma((4,)),
            dma((chips,)),
        ],
        compiler_params=pltpu.CompilerParams(
            collective_id=0, has_side_effects=True, vmem_limit_bytes=52 * 1024 * 1024
        ),
        cost_estimate=pl.CostEstimate(flops=2 * rows * channels * channels, bytes_accessed=20_000_000, transcendentals=0),
    )(tokens, projected, short_filter, long_filter, conv_bias.reshape(1, -1), out_weight)


def shifted(block, axis, distance):
    devices = range(lax.axis_size(axis))
    route = [(i - distance, i) for i in devices if i - distance in devices]
    return lax.ppermute(block, axis, route)


def general(tokens, projected, short_filter, long_filter, conv_bias, out_weight):
    rows, channels = tokens.shape[0], out_weight.shape[0]
    groups, taps = long_filter.shape
    edge = shifted(projected[rows - 2 :], "ctx", 1)
    source = jnp.concatenate([edge, projected], axis=0).astype(F32)
    mixed = short_filter[0] * source[2:] + short_filter[1] * source[1:-1] + short_filter[2] * source[:-2]
    carried = (mixed[:, channels : 2 * channels] * mixed[:, 2 * channels :]).astype(BF16)
    extended = jnp.concatenate([shifted(carried[rows - taps + 1 :], "ctx", 1), carried], axis=0)
    block = min(128, rows)
    width = block + taps - 1
    pattern = jnp.concatenate([long_filter[:, ::-1], jnp.zeros((groups, block), BF16)], axis=1)
    toeplitz = jnp.tile(pattern, (1, block))[:, : block * width].reshape(groups, block, width)
    grouped = extended.reshape(extended.shape[0], groups, -1)

    def one_block(index):
        window = lax.dynamic_slice_in_dim(grouped, index * block, width, 0)
        return jnp.einsum("gts,sgc->tgc", toeplitz, window, preferred_element_type=F32).reshape(block, -1)

    conv = lax.map(one_block, jnp.arange(rows // block, dtype=jnp.int32)).reshape(rows, -1)
    gated = (mixed[:, :channels] * (conv + conv_bias * carried.astype(F32))).astype(BF16)
    whole = lax.all_gather(out_weight, "ctx", axis=1, tiled=True)
    branch = jnp.dot(gated, whole, preferred_element_type=F32)
    return (tokens.astype(F32) + branch).astype(BF16)


def solution(mesh):
    fits = mesh.shape["groups"] == 2 and mesh.shape["ctx"] == 16
    placed = (P(("groups", "ctx"), None), P(("groups", "ctx"), None), P(), P(), P(), P(None, "ctx"))
    return jax.shard_map(
        on_device if fits else general,
        mesh=mesh, in_specs=placed, out_specs=P(("groups", "ctx"), None), check_vma=False,
    )
```

```python
import functools

import jax
import jax.numpy as jnp
from jax import lax
from jax.experimental import pallas as pl
from jax.experimental.pallas import tpu as pltpu
from jax.sharding import PartitionSpec as P

F32 = jnp.float32
BF16 = jnp.bfloat16
MESH = pl.DeviceIdType.MESH
LANES = 128
CHUNK = 256
EDGE = 16
SIDE = 608


def layer_kernel(
    tok, proj, sf_in, lf_in, cb_in, w, out,
    pv, xv, xr, tv, hr, wv, gv, tk, ob, sf, lf, cb,
    ring_s, ring_r, x_s, x_r, sib_s, sib_r, halo_s, halo_r, loc, out_s,
):
    rows, channels = tok.shape[0], w.shape[0]
    taps = lf.shape[1]
    chunks = channels // CHUNK
    middle = channels - 2 * SIDE
    shard = w.shape[1]

    grp = lax.axis_index("groups")
    me = lax.axis_index("ctx")
    devices = lax.axis_size("ctx")
    core = me % 2
    chip = me // 2
    ring = devices // 2
    depth = ring // 2
    cz, cy = chip // 2, chip % 2
    pos = cz * (1 - cy) + (ring - 1 - cz) * cy

    def chip_at(position):
        q = (position + ring) % ring
        qy = q // depth
        qz = q * (1 - qy) + (ring - 1 - q) * qy
        return qz * 2 + qy

    def device_at(position):
        return chip_at(position) * 2 + core

    right = (grp, device_at(pos + 1))
    left = (grp, device_at(pos - 1))
    across = (1 - grp, me)
    sibling = (grp, me + 1 - 2 * core)
    following = (grp, (me + 1) % devices)
    previous = (grp, (me + devices - 1) % devices)
    has_next = me < devices - 1
    has_prev = me > 0

    tail = taps + EDGE
    head = rows - tail
    load_tail = pltpu.make_async_copy(proj.at[pl.ds(head, tail)], pv.at[pl.ds(EDGE + head, tail)], loc.at[0])
    load_head = pltpu.make_async_copy(proj.at[pl.ds(0, head)], pv.at[pl.ds(EDGE, head)], loc.at[1])
    load_tok = pltpu.make_async_copy(tok, tk, loc.at[2])
    load_w = pltpu.make_async_copy(w, wv.at[me], loc.at[3])
    load_sf = pltpu.make_async_copy(sf_in, sf, loc.at[4])
    load_lf = pltpu.make_async_copy(lf_in, lf, loc.at[5])
    load_cb = pltpu.make_async_copy(cb_in, cb, loc.at[6])
    load_sf.start()
    load_lf.start()
    load_tail.start()
    load_cb.start()
    load_head.start()
    load_w.start()
    load_tok.start()

    barrier = pltpu.get_barrier_semaphore()
    for other in (left, right, across, sibling, following, previous):
        pl.semaphore_signal(barrier, inc=1, device_id=other, device_id_type=MESH)
    pl.semaphore_wait(barrier, 6)

    def remote(src, dst, ssem, rsem, dev):
        return pltpu.make_async_remote_copy(
            src_ref=src, dst_ref=dst, send_sem=ssem, recv_sem=rsem, device_id=dev, device_id_type=MESH
        )

    def span(step, d, piece):
        size = middle if piece == 1 else SIDE
        if piece == 0:
            start = grp * (SIDE + middle)
        elif piece == 1:
            start = SIDE
        else:
            start = (1 - grp) * (SIDE + middle)
        if step == depth:
            size = size // 2
            start = start + d * size
        return pl.ds(pl.multiple_of(start, EDGE), size)

    def owner(step, d):
        return device_at(pos - step) if d == 0 else device_at(pos + step)

    def ring_copy(step, d, piece):
        own = owner(step - 1, d)
        sp = span(step, d, piece)
        i = (step - 1) * 4 + d * 2 + piece
        src = w.at[sp] if step == 1 else wv.at[own, sp]
        return remote(src, wv.at[own, sp], ring_s.at[i], ring_r.at[i], right if d == 0 else left)

    def across_copy(step, d, piece=0):
        own = owner(step, d)
        sp = span(step, d, piece)
        i = (step - 1) * 2 + d
        return remote(wv.at[own, sp], wv.at[own, sp], x_s.at[i], x_r.at[i], across)

    def sibling_copy(step, d, piece):
        own = owner(step, d)
        sp = span(step, d, piece)
        i = (step - 1) * 6 + d * 3 + piece
        return remote(wv.at[own, sp], wv.at[own, sp], sib_s.at[i], sib_r.at[i], sibling)

    own_sib = remote(w, wv.at[me], sib_s.at[depth * 6], sib_r.at[depth * 6], sibling)
    edge_copy = remote(
        proj.at[pl.ds(rows - EDGE, EDGE)], pv.at[pl.ds(0, EDGE)], halo_s.at[0], halo_r.at[0], following
    )
    halo_copy = remote(
        xv.at[pl.ds(rows, taps)], xv.at[pl.ds(0, taps)], halo_s.at[1], halo_r.at[1], following
    )

    def ring_arrival(step, d, piece):
        own = owner(step, d)
        sp = span(step, d, piece)
        i = (step - 1) * 4 + d * 2 + piece
        remote(wv.at[own, sp], wv.at[own, sp], ring_s.at[i], ring_r.at[i], right).wait_recv()
        if step < depth:
            ring_copy(step + 1, d, piece).start()
        if piece == 0:
            across_copy(step, d).start()
        sibling_copy(step, d, piece).start()

    def across_arrival(step, d):
        across_copy(step, d, 2).wait_recv()
        sibling_copy(step, d, 2).start()

    @pl.when(has_next)
    def _():
        edge_copy.start()

    for piece in (0, 1):
        for d in (0, 1):
            ring_copy(1, d, piece).start()
    own_sib.start()

    def ring_both(step, piece):
        ring_arrival(step, 0, piece)
        ring_arrival(step, 1, piece)

    def across_both(step):
        across_arrival(step, 0)
        across_arrival(step, 1)

    def at(index, k, *events):
        @pl.when(k == index)
        def _():
            for fn, *args in events:
                fn(*args)

    def mix(r0, count, c0, width):
        cols = pl.ds(pl.multiple_of(c0, LANES), width)
        x = pv[pl.ds(pl.multiple_of(r0, EDGE), count + EDGE), cols].astype(F32)
        total = sf[0:1, cols] * x[EDGE:]
        total = total + sf[1:2, cols] * x[EDGE - 1 : -1]
        return total + sf[2:3, cols] * x[EDGE - 2 : -2]

    strip = 64

    def carry_strip(r0, c0):
        prod = mix(r0, strip, channels + c0, LANES) * mix(r0, strip, 2 * channels + c0, LANES)
        at_rows = pl.ds(pl.multiple_of(taps + r0, EDGE), strip)
        cols = pl.ds(pl.multiple_of(c0, LANES), LANES)
        xv[at_rows, cols] = prod.astype(BF16)
        xr[at_rows, cols] = pltpu.roll(prod, LANES // 2, 1).astype(BF16)

    load_sf.wait()
    load_lf.wait()
    load_cb.wait()
    load_tail.wait()
    tiles = channels // LANES

    @pl.loop(0, tiles)
    def _(t):
        for r in range(rows - taps, rows, strip):
            carry_strip(r, t * LANES)

    @pl.when(has_next)
    def _():
        halo_copy.start()

    jj = lax.broadcasted_iota(jnp.int32, (taps, 2 * taps), 0)
    ss = lax.broadcasted_iota(jnp.int32, (taps, 2 * taps), 1)
    flip = jnp.where(ss == taps - jj, 1.0, 0.0).astype(BF16)
    hr[...] = jnp.dot(lf[...], flip, preferred_element_type=F32)

    @pl.when(me == 0)
    def _():
        pv[0:EDGE, :] = jnp.zeros((EDGE, pv.shape[1]), BF16)
        xv[0:taps, :] = jnp.zeros((taps, channels), BF16)

    @pl.when(has_prev)
    def _():
        edge_copy.wait_recv()

    load_head.wait()

    def build_taps(g):
        row = jnp.broadcast_to(hr[pl.ds(g, 1), :], (taps, 2 * taps))
        mat = pltpu.roll(row, 0, 1, stride=1, stride_axis=0)
        tv[pl.ds(pl.multiple_of(g * taps, taps), taps), :] = mat.astype(BF16)

    per_tile = lf.shape[0] // tiles

    @pl.loop(0, tiles)
    def _(t):
        for r in range(0, rows - taps, strip):
            carry_strip(r, t * LANES)

        @pl.loop(0, per_tile)
        def _(i):
            build_taps(t * per_tile + i)

        at(7, t, (ring_both, 1, 0))
        at(13, t, (ring_both, 1, 1))

    @pl.when(has_prev)
    def _():
        halo_copy.wait_recv()

    half = LANES // 2
    quarter = per_tile // 2
    gw = half // quarter
    pairs = rows // (2 * taps)
    low = lax.broadcasted_iota(jnp.int32, (1, LANES), 1) < half

    def conv_tile(t):
        c0 = t * LANES
        cols = pl.ds(pl.multiple_of(c0, LANES), LANES)
        lows, highs = [], []
        for j in range(pairs):
            a = xv[pl.ds(j * 2 * taps, 2 * taps), cols]
            b = xr[pl.ds(j * 2 * taps + taps, 2 * taps), cols]
            lows.append(jnp.where(low, a, b))
            highs.append(jnp.where(low, b, a))
        parts = []
        lane = lax.broadcasted_iota(jnp.int32, (1, pairs * LANES), 1)
        which = (lane % half) // gw
        for side, blocks in enumerate((lows, highs)):
            rhs = jnp.concatenate(blocks, axis=1)
            first = (t * per_tile + side * quarter) * taps
            res = jnp.dot(
                tv[pl.ds(pl.multiple_of(first, taps), quarter * taps), :], rhs, preferred_element_type=F32
            )
            total = res[0:taps]
            for i in range(1, quarter):
                total = jnp.where(which == i, res[i * taps : (i + 1) * taps], total)
            parts.append(total)
        for j in range(pairs):
            z1 = parts[0][:, j * LANES : (j + 1) * LANES]
            z2 = parts[1][:, j * LANES : (j + 1) * LANES]
            even = jnp.where(low, z1, z2)
            odd = pltpu.roll(jnp.where(low, z2, z1), half, 1)
            for b, conv in ((2 * j, even), (2 * j + 1, odd)):
                r0 = b * taps
                carried = xv[pl.ds(taps + r0, taps), cols].astype(F32)
                gate = mix(r0, taps, c0, LANES)
                gv[pl.ds(r0, taps), cols] = (gate * (conv + cb[0:1, cols] * carried)).astype(BF16)

    @pl.loop(0, tiles)
    def _(t):
        conv_tile(t)
        at(1, t, (across_both, 1))
        at(4, t, (ring_both, 2, 0))
        at(8, t, (ring_both, 2, 1))
        at(11, t, (across_both, 2))
        at(14, t, (ring_both, 3, 0))

    load_tok.wait()
    load_w.wait()

    def sibling_wait(step, d):
        for piece in range(3):
            sibling_copy(step, d, piece).wait_recv()

    blocks = ring
    width = 2 * shard

    def out_copy(idx):
        sign = 1 - 2 * (idx % 2)
        c = chip_at(pos + ((idx + 1) // 2) * sign)
        cols = pl.ds(pl.multiple_of(c * width, width), width)
        return pltpu.make_async_copy(ob.at[:, cols], out.at[:, cols], out_s.at[idx])

    @pl.loop(0, blocks)
    def _(idx):
        at(0, idx, (own_sib.wait_recv,))
        at(1, idx, (sibling_wait, 1, 0))
        at(2, idx, (sibling_wait, 1, 1), (ring_both, 3, 1))
        at(3, idx, (sibling_wait, 2, 0))
        at(4, idx, (sibling_wait, 2, 1), (across_both, 3), (ring_both, 4, 0), (ring_both, 4, 1))
        at(5, idx, (sibling_wait, 3, 0))
        at(6, idx, (sibling_wait, 3, 1), (across_both, 4))
        at(7, idx, (sibling_wait, depth, 0), (sibling_wait, depth, 1))
        sign = 1 - 2 * (idx % 2)
        c = chip_at(pos + ((idx + 1) // 2) * sign)
        cols = pl.ds(pl.multiple_of(c * width, width), width)

        rhs = jnp.concatenate([wv[2 * c], wv[2 * c + 1]], axis=1)
        branch = jnp.dot(gv[...], rhs, preferred_element_type=F32)
        ob[:, cols] = (tk[:, cols].astype(F32) + branch).astype(BF16)
        out_copy(idx).start()

    for step in range(1, depth + 1):
        for d in (0, 1):
            ring_copy(step, d, 0).wait_send()
            ring_copy(step, d, 1).wait_send()
            across_copy(step, d).wait_send()
            for piece in range(3):
                sibling_copy(step, d, piece).wait_send()
    own_sib.wait_send()

    @pl.when(has_next)
    def _():
        edge_copy.wait_send()
        halo_copy.wait_send()

    for idx in range(blocks):
        out_copy(idx).wait()


def on_device(tokens, projected, short_filter, long_filter, conv_bias, out_weight):
    rows, channels = tokens.shape[0], out_weight.shape[0]
    taps = long_filter.shape[1]
    devices = lax.axis_size("ctx")
    chips = devices // 2
    depth = chips // 2
    anyspace = pl.BlockSpec(memory_space=pl.ANY)
    dma = pltpu.SemaphoreType.DMA
    return pl.pallas_call(
        layer_kernel,
        out_shape=jax.ShapeDtypeStruct(tokens.shape, BF16),
        in_specs=[anyspace] * 6,
        out_specs=anyspace,
        scratch_shapes=[
            pltpu.VMEM((rows + EDGE, projected.shape[1]), BF16),
            pltpu.VMEM((rows + taps, channels), BF16),
            pltpu.VMEM((rows + taps, channels), BF16),
            pltpu.VMEM((long_filter.shape[0] * taps, 2 * taps), BF16),
            pltpu.VMEM((long_filter.shape[0], 2 * taps), F32),
            pltpu.VMEM((devices, channels, out_weight.shape[1]), BF16),
            pltpu.VMEM((rows, channels), BF16),
            pltpu.VMEM(tokens.shape, BF16),
            pltpu.VMEM(tokens.shape, BF16),
            pltpu.VMEM(short_filter.shape, F32),
            pltpu.VMEM(long_filter.shape, BF16),
            pltpu.VMEM((1, channels), F32),
            dma((depth * 4,)),
            dma((depth * 4,)),
            dma((depth * 2,)),
            dma((depth * 2,)),
            dma((depth * 6 + 1,)),
            dma((depth * 6 + 1,)),
            dma((2,)),
            dma((2,)),
            dma((7,)),
            dma((chips,)),
        ],
        compiler_params=pltpu.CompilerParams(
            collective_id=0, has_side_effects=True, vmem_limit_bytes=63 * 1024 * 1024
        ),
        cost_estimate=pl.CostEstimate(flops=2 * rows * channels * channels, bytes_accessed=20_000_000, transcendentals=0),
    )(tokens, projected, short_filter, long_filter, conv_bias.reshape(1, -1), out_weight)


def shifted(block, axis, distance):
    devices = range(lax.axis_size(axis))
    route = [(i - distance, i) for i in devices if i - distance in devices]
    return lax.ppermute(block, axis, route)


def general(tokens, projected, short_filter, long_filter, conv_bias, out_weight):
    rows, channels = tokens.shape[0], out_weight.shape[0]
    groups, taps = long_filter.shape
    edge = shifted(projected[rows - 2 :], "ctx", 1)
    source = jnp.concatenate([edge, projected], axis=0).astype(F32)
    mixed = short_filter[0] * source[2:] + short_filter[1] * source[1:-1] + short_filter[2] * source[:-2]
    carried = (mixed[:, channels : 2 * channels] * mixed[:, 2 * channels :]).astype(BF16)
    extended = jnp.concatenate([shifted(carried[rows - taps + 1 :], "ctx", 1), carried], axis=0)
    block = min(128, rows)
    width = block + taps - 1
    pattern = jnp.concatenate([long_filter[:, ::-1], jnp.zeros((groups, block), BF16)], axis=1)
    toeplitz = jnp.tile(pattern, (1, block))[:, : block * width].reshape(groups, block, width)
    grouped = extended.reshape(extended.shape[0], groups, -1)

    def one_block(index):
        window = lax.dynamic_slice_in_dim(grouped, index * block, width, 0)
        return jnp.einsum("gts,sgc->tgc", toeplitz, window, preferred_element_type=F32).reshape(block, -1)

    conv = lax.map(one_block, jnp.arange(rows // block, dtype=jnp.int32)).reshape(rows, -1)
    gated = (mixed[:, :channels] * (conv + conv_bias * carried.astype(F32))).astype(BF16)
    whole = lax.all_gather(out_weight, "ctx", axis=1, tiled=True)
    branch = jnp.dot(gated, whole, preferred_element_type=F32)
    return (tokens.astype(F32) + branch).astype(BF16)


def solution(mesh):
    fits = mesh.shape["groups"] == 2 and mesh.shape["ctx"] == 16
    placed = (P(("groups", "ctx"), None), P(("groups", "ctx"), None), P(), P(), P(), P(None, "ctx"))
    return jax.shard_map(
        on_device if fits else general,
        mesh=mesh, in_specs=placed, out_specs=P(("groups", "ctx"), None), check_vma=False,
    )
```
